32 devices in a mesh: gx: 4 (over y, core), gy: 8 (over z, x).
Axes of the slice: x: 2, y: 2, z: 4, core: 2. Of those that a mesh axis runs over, the one named last changes fastest.
Arguments:
- skip_input: bfloat16 [32, 16, 2048], P(None, 'gx', 'gy'), may hold values from -6 to 6
- w_encoder: bfloat16 [64, 864], replicated, may hold values from -0.625 to 0.625
- w_bottom: bfloat16 [128, 1728], P('gx'), may hold values from -0.3125 to 0.3125
- w_middle: bfloat16 [64, 5184], replicated, may hold values from -0.15625 to 0.15625
- w_upper: bfloat16 [32, 2592], replicated, may hold values from -0.21875 to 0.21875
- cotangent: bfloat16 [32, 16, 2048], P(None, 'gx', 'gy'), may hold values from -6 to 6
Outputs:
- features: bfloat16 [32, 16, 2048], P(None, 'gx', 'gy')
- grad_skip: bfloat16 [32, 16, 2048], P(None, 'gx', 'gy')
- grad_encoder: float32 [64, 864], replicated
- grad_bottom: float32 [128, 1728], P('gx')
- grad_middle: float32 [64, 5184], replicated
- grad_upper: float32 [32, 2592], replicated
The draws below stay inside these ranges and needn't reach their ends.
All inputs are finite; a program needn't handle non-finite values.
Results may differ from the reference program's by a relative error of at most 0.017.
Values may be sent and summed in bfloat16 or wider, within the bound.
A program may use at most 64 MiB of HBM per device.

```python
import math
import jax
import jax.numpy as jnp
from jax import lax

C0 = 32
C1 = 64
C2 = 128
Z = 16
X0 = 16
Y0 = 128


def levels(stream_key, extent, pieces, low, top_value):
    factor_of = 1.0
    for position, blocks in pieces:
        steps = jax.random.uniform(jax.random.fold_in(jax.random.fold_in(stream_key, 6), position), (blocks,), jnp.float32, low / len(pieces), top_value / len(pieces))
        factor_of = factor_of * jnp.repeat(jnp.exp(steps), extent[position] // blocks).reshape((-1,) + (1,) * (len(extent) - 1 - position))
    return factor_of


def noise(stream_key, shape, width, bound, shards=(), held_as=jnp.bfloat16):
    entries = jax.random.normal(stream_key, shape, jnp.float32) * width
    if len(shards) > 0:
        entries = levels(stream_key, shape, shards, -0.22, 0.18) * entries
    return jnp.clip(entries, min=-bound, max=bound).astype(held_as)


def setup_inputs(seed: int = 0) -> dict:
    splits = jax.random.split(jax.random.key(seed), 7)
    return {
        "skip_input": noise(splits[0], (C0, X0, Y0 * Z), 1.0, 6.0, ((1, 4), (2, 8))),
        "w_encoder": noise(splits[1], (C1, 27 * C0), (27 * C0 // 8) ** -0.5, 0.625),
        "w_bottom": noise(splits[2], (C2, 27 * C1), (27 * C1 // 4) ** -0.5, 0.3125, ((0, 4),)),
        "w_middle": noise(splits[3], (C1, 27 * (C2 + C1)), (27 * C1) ** -0.5, 0.15625),
        "w_upper": noise(splits[4], (C0, 27 * (C1 + C0)), (27 * C0) ** -0.5, 0.21875),
        "cotangent": noise(splits[5], (C0, X0, Y0 * Z), 1.0, 6.0, ((1, 4), (2, 8))),
    }


def z_shift(extended, z_step, z_depth):
    length = extended.shape[2]
    padded = jnp.pad(extended, ((0, 0), (0, 0), (1, 1)))
    shifted = padded[:, :, 1 + z_step:1 + z_step + length]
    z_index = lax.broadcasted_iota(jnp.int32, (1, 1, length), 2) % z_depth + z_step
    inside = (z_index >= 0) & (z_index < z_depth)
    return jnp.where(inside, shifted, jnp.zeros_like(shifted))

def tap_piece(shifted_set, a, b, c, row_count, col_count, z_depth, flipped):
    x_off, y_off, z_off = (2 - a, 2 - b, 2 - c) if flipped else (a, b, c)
    source = shifted_set[z_off]
    tap_slice = source[:, x_off:x_off + row_count, y_off * z_depth:(y_off + col_count) * z_depth]
    return tap_slice.reshape(source.shape[0], row_count * col_count * z_depth)

def conv_forward(extended, weight, row_count, col_count, z_depth):
    in_chan = extended.shape[0]
    shifted_set = [z_shift(extended, z_step, z_depth) for z_step in (-1, 0, 1)]
    total_sum = jnp.zeros((weight.shape[0], row_count * col_count * z_depth), jnp.float32)
    for a in range(3):
        for b in range(3):
            for c in range(3):
                tap_number = 9 * a + 3 * b + c
                total_sum = total_sum + jnp.dot(weight[:, tap_number * in_chan:(tap_number + 1) * in_chan], tap_piece(shifted_set, a, b, c, row_count, col_count, z_depth, False), preferred_element_type=jnp.float32)
    return total_sum

def conv_backward(extended, weight, row_count, col_count, z_depth):
    in_chan = weight.shape[1] // 27
    shifted_set = [z_shift(extended, z_step, z_depth) for z_step in (-1, 0, 1)]
    total_sum = jnp.zeros((in_chan, row_count * col_count * z_depth), jnp.float32)
    for a in range(3):
        for b in range(3):
            for c in range(3):
                tap_number = 9 * a + 3 * b + c
                total_sum = total_sum + lax.dot_general(weight[:, tap_number * in_chan:(tap_number + 1) * in_chan], tap_piece(shifted_set, a, b, c, row_count, col_count, z_depth, True), (((0,), (0,)), ((), ())), preferred_element_type=jnp.float32)
    return total_sum

def weight_grad(extended, error_flat, row_count, col_count, z_depth):
    shifted_set = [z_shift(extended, z_step, z_depth) for z_step in (-1, 0, 1)]
    blocks = []
    for a in range(3):
        for b in range(3):
            for c in range(3):
                blocks.append(lax.dot_general(error_flat, tap_piece(shifted_set, a, b, c, row_count, col_count, z_depth, False), (((1,), (1,)), ((), ())), preferred_element_type=jnp.float32))
    return jnp.concatenate(blocks, axis=1)

def pool_mean(values, z_depth):
    channels, row_count, length = values.shape
    col_count = length // z_depth
    shaped = values.astype(jnp.float32).reshape(channels, row_count // 2, 2, col_count // 2, 2, z_depth // 2, 2)
    return shaped.mean(axis=(2, 4, 6)).reshape(channels, row_count // 2, col_count // 2 * (z_depth // 2))

def block_sum(values, z_depth):
    channels, row_count, length = values.shape
    col_count = length // z_depth
    shaped = values.reshape(channels, row_count // 2, 2, col_count // 2, 2, z_depth // 2, 2)
    return shaped.sum(axis=(2, 4, 6)).reshape(channels, row_count // 2, col_count // 2 * (z_depth // 2))

def upsample(values, z_depth):
    channels, row_count, length = values.shape
    col_count = length // z_depth
    shaped = values.reshape(channels, row_count, 1, col_count, 1, z_depth, 1)
    shaped = jnp.broadcast_to(shaped, (channels, row_count, 2, col_count, 2, z_depth, 2))
    return shaped.reshape(channels, 2 * row_count, 4 * col_count * z_depth)

def silu_slope(values):
    s_value = jax.nn.sigmoid(values)
    return s_value * (1.0 + values * (1.0 - s_value))

def pad_grid(values, z_depth):
    return jnp.pad(values, ((0, 0), (1, 1), (z_depth, z_depth)))

def reference(skip_input, w_encoder, w_bottom, w_middle, w_upper, cotangent):
    rows_fine, cols_fine = (X0, Y0)
    rows_mid, cols_mid, depth_mid = (X0 // 2, Y0 // 2, Z // 2)
    rows_low, cols_low, depth_low = (X0 // 4, Y0 // 4, Z // 4)
    cells_fine = X0 * Y0 * Z
    scale_fine = 1.0 / math.sqrt(cells_fine)
    scale_mid = 1.0 / math.sqrt(cells_fine // 8)
    scale_low = 1.0 / math.sqrt(cells_fine // 64)
    pool_top = pool_mean(skip_input, Z).astype(jnp.bfloat16)
    ext_pool = pad_grid(pool_top, depth_mid)
    pre_one = conv_forward(ext_pool, w_encoder, rows_mid, cols_mid, depth_mid)
    act_one = jax.nn.silu(pre_one).astype(jnp.bfloat16).reshape(-1, rows_mid, cols_mid * depth_mid)
    pool_mid = pool_mean(act_one, depth_mid).astype(jnp.bfloat16)
    ext_low = pad_grid(pool_mid, depth_low)
    pre_two = conv_forward(ext_low, w_bottom, rows_low, cols_low, depth_low)
    act_two = jax.nn.silu(pre_two).astype(jnp.bfloat16).reshape(-1, rows_low, cols_low * depth_low)
    cat_mid = jnp.concatenate([upsample(act_two, depth_low), act_one], axis=0)
    ext_mid = pad_grid(cat_mid, depth_mid)
    pre_three = conv_forward(ext_mid, w_middle, rows_mid, cols_mid, depth_mid)
    act_three = jax.nn.silu(pre_three).astype(jnp.bfloat16).reshape(-1, rows_mid, cols_mid * depth_mid)
    cat_top = jnp.concatenate([upsample(act_three, depth_mid), skip_input], axis=0)
    ext_top = pad_grid(cat_top, Z)
    pre_four = conv_forward(ext_top, w_upper, rows_fine, cols_fine, Z)
    top_chan = skip_input.shape[0]
    features = jax.nn.silu(pre_four).astype(jnp.bfloat16).reshape(top_chan, rows_fine, cols_fine * Z)
    err_four = (cotangent.reshape(top_chan, -1).astype(jnp.float32) * silu_slope(pre_four)).astype(jnp.bfloat16)
    grad_upper = weight_grad(ext_top, err_four, rows_fine, cols_fine, Z) * scale_fine
    dcat_top = conv_backward(pad_grid(err_four.reshape(top_chan, rows_fine, cols_fine * Z), Z), w_upper, rows_fine, cols_fine, Z).reshape(-1, rows_fine, cols_fine * Z)
    mid_chan = act_three.shape[0]
    err_three = (block_sum(dcat_top[:mid_chan], Z).reshape(mid_chan, -1) * silu_slope(pre_three)).astype(jnp.bfloat16)
    grad_middle = weight_grad(ext_mid, err_three, rows_mid, cols_mid, depth_mid) * scale_mid
    dcat_mid = conv_backward(pad_grid(err_three.reshape(mid_chan, rows_mid, cols_mid * depth_mid), depth_mid), w_middle, rows_mid, cols_mid, depth_mid).reshape(-1, rows_mid, cols_mid * depth_mid)
    low_chan = act_two.shape[0]
    err_two = (block_sum(dcat_mid[:low_chan], depth_mid).reshape(low_chan, -1) * silu_slope(pre_two)).astype(jnp.bfloat16)
    grad_bottom = weight_grad(ext_low, err_two, rows_low, cols_low, depth_low) * scale_low
    dpool_mid = conv_backward(pad_grid(err_two.reshape(low_chan, rows_low, cols_low * depth_low), depth_low), w_bottom, rows_low, cols_low, depth_low).reshape(-1, rows_low, cols_low * depth_low)
    dact_one = dcat_mid[low_chan:] + upsample(dpool_mid, depth_low) / 8.0
    err_one = (dact_one.reshape(mid_chan, -1) * silu_slope(pre_one)).astype(jnp.bfloat16)
    grad_encoder = weight_grad(ext_pool, err_one, rows_mid, cols_mid, depth_mid) * scale_mid
    dpool_top = conv_backward(pad_grid(err_one.reshape(mid_chan, rows_mid, cols_mid * depth_mid), depth_mid), w_encoder, rows_mid, cols_mid, depth_mid).reshape(-1, rows_mid, cols_mid * depth_mid)
    grad_skip = (dcat_top[mid_chan:] + upsample(dpool_top, depth_mid) / 8.0).astype(jnp.bfloat16)
    return (features, grad_skip, grad_encoder, grad_bottom, grad_middle, grad_upper)
```

```python
import math

import jax
import jax.numpy as jnp
from jax import lax
from jax.sharding import PartitionSpec as P

Z = 16


def extended_2(cells, sides, width):
    for axis, dim in sides:
        count = lax.axis_size(axis)
        ends = count - 1
        head = lax.slice_in_dim(cells, 0, width, axis=dim)
        tail = lax.slice_in_dim(cells, cells.shape[dim] - width, cells.shape[dim], axis=dim)
        cells = jnp.concatenate(
            [
                lax.ppermute(tail, axis, [(i, (i + 1) % count) for i in range(ends)]),
                cells,
                lax.ppermute(head, axis, [((i + 1) % count, i) for i in range(ends)]),
            ],
            axis=dim,
        )
    return cells


def z_shift(extended, z_step, z_depth):
    length = extended.shape[2]
    padded = jnp.pad(extended, ((0, 0), (0, 0), (1, 1)))
    shifted = padded[:, :, 1 + z_step : 1 + z_step + length]
    z_index = lax.broadcasted_iota(jnp.int32, (1, 1, length), 2) % z_depth + z_step
    inside = (z_index >= 0) & (z_index < z_depth)
    return jnp.where(inside, shifted, jnp.zeros_like(shifted))


def tap_piece(shifted_set, a, b, c, row_count, col_count, z_depth, flipped):
    x_off, y_off, z_off = (2 - a, 2 - b, 2 - c) if flipped else (a, b, c)
    source = shifted_set[z_off]
    tap_slice = source[
        :, x_off : x_off + row_count, y_off * z_depth : (y_off + col_count) * z_depth
    ]
    return tap_slice.reshape(source.shape[0], row_count * col_count * z_depth)


def conv_forward(extended, weight, row_count, col_count, z_depth):
    in_chan = extended.shape[0]
    shifted_set = [z_shift(extended, z_step, z_depth) for z_step in (-1, 0, 1)]
    total_sum = jnp.zeros((weight.shape[0], row_count * col_count * z_depth), jnp.float32)
    for a in range(3):
        for b in range(3):
            for c in range(3):
                tap_number = 9 * a + 3 * b + c
                total_sum = total_sum + jnp.dot(
                    weight[:, tap_number * in_chan : (tap_number + 1) * in_chan],
                    tap_piece(shifted_set, a, b, c, row_count, col_count, z_depth, False),
                    preferred_element_type=jnp.float32,
                )
    return total_sum


def conv_backward(extended, weight, row_count, col_count, z_depth):
    in_chan = weight.shape[1] // 27
    shifted_set = [z_shift(extended, z_step, z_depth) for z_step in (-1, 0, 1)]
    total_sum = jnp.zeros((in_chan, row_count * col_count * z_depth), jnp.float32)
    for a in range(3):
        for b in range(3):
            for c in range(3):
                tap_number = 9 * a + 3 * b + c
                total_sum = total_sum + lax.dot_general(
                    weight[:, tap_number * in_chan : (tap_number + 1) * in_chan],
                    tap_piece(shifted_set, a, b, c, row_count, col_count, z_depth, True),
                    (((0,), (0,)), ((), ())),
                    preferred_element_type=jnp.float32,
                )
    return total_sum


def weight_grad(extended, error_flat, row_count, col_count, z_depth):
    shifted_set = [z_shift(extended, z_step, z_depth) for z_step in (-1, 0, 1)]
    blocks = []
    for a in range(3):
        for b in range(3):
            for c in range(3):
                blocks.append(
                    lax.dot_general(
                        error_flat,
                        tap_piece(shifted_set, a, b, c, row_count, col_count, z_depth, False),
                        (((1,), (1,)), ((), ())),
                        preferred_element_type=jnp.float32,
                    )
                )
    return jnp.concatenate(blocks, axis=1)


def pool_mean(values, z_depth):
    channels, row_count, length = values.shape
    col_count = length // z_depth
    shaped = values.astype(jnp.float32).reshape(
        channels, row_count // 2, 2, col_count // 2, 2, z_depth // 2, 2
    )
    return shaped.mean(axis=(2, 4, 6)).reshape(
        channels, row_count // 2, col_count // 2 * (z_depth // 2)
    )


def block_sum(values, z_depth):
    channels, row_count, length = values.shape
    col_count = length // z_depth
    shaped = values.reshape(channels, row_count // 2, 2, col_count // 2, 2, z_depth // 2, 2)
    return shaped.sum(axis=(2, 4, 6)).reshape(
        channels, row_count // 2, col_count // 2 * (z_depth // 2)
    )


def upsample(values, z_depth):
    channels, row_count, length = values.shape
    col_count = length // z_depth
    shaped = values.reshape(channels, row_count, 1, col_count, 1, z_depth, 1)
    shaped = jnp.broadcast_to(shaped, (channels, row_count, 2, col_count, 2, z_depth, 2))
    return shaped.reshape(channels, 2 * row_count, 4 * col_count * z_depth)


def silu_slope(values):
    s_value = jax.nn.sigmoid(values)
    return s_value * (1.0 + values * (1.0 - s_value))


def spatial_halo(values, z_depth):
    widened = extended_2(values, (("gy", 2),), z_depth)
    return extended_2(widened, (("gx", 1),), 1)


def per_device(skip_input, w_encoder, w_bottom, w_middle, w_upper, cotangent):
    top_chan = skip_input.shape[0]
    rows_fine = skip_input.shape[1]
    cols_fine = skip_input.shape[2] // Z
    rows_mid, cols_mid, depth_mid = (rows_fine // 2, cols_fine // 2, Z // 2)
    rows_low, cols_low, depth_low = (rows_fine // 4, cols_fine // 4, Z // 4)
    cells_fine = rows_fine * cols_fine * Z * lax.axis_size("gx") * lax.axis_size("gy")
    scale_fine = 1.0 / math.sqrt(cells_fine)
    scale_mid = 1.0 / math.sqrt(cells_fine // 8)
    scale_low = 1.0 / math.sqrt(cells_fine // 64)
    pool_top = pool_mean(skip_input, Z).astype(jnp.bfloat16)
    ext_pool = spatial_halo(pool_top, depth_mid)
    pre_one = conv_forward(ext_pool, w_encoder, rows_mid, cols_mid, depth_mid)
    act_one = jax.nn.silu(pre_one).astype(jnp.bfloat16).reshape(-1, rows_mid, cols_mid * depth_mid)
    pool_mid = pool_mean(act_one, depth_mid).astype(jnp.bfloat16)
    col_ext = extended_2(pool_mid, (("gy", 2),), depth_low)
    whole_rows = lax.all_gather(col_ext, "gx", axis=1, tiled=True)
    ext_low = jnp.pad(whole_rows, ((0, 0), (1, 1), (0, 0)))
    rows_all = whole_rows.shape[1]
    pre_two = conv_forward(ext_low, w_bottom, rows_all, cols_low, depth_low)
    act_block = (
        jax.nn.silu(pre_two).astype(jnp.bfloat16).reshape(-1, rows_all, cols_low * depth_low)
    )
    act_two = lax.all_to_all(act_block, "gx", split_axis=1, concat_axis=0, tiled=True)
    cat_mid = jnp.concatenate([upsample(act_two, depth_low), act_one], axis=0)
    ext_mid = spatial_halo(cat_mid, depth_mid)
    pre_three = conv_forward(ext_mid, w_middle, rows_mid, cols_mid, depth_mid)
    act_three = (
        jax.nn.silu(pre_three).astype(jnp.bfloat16).reshape(-1, rows_mid, cols_mid * depth_mid)
    )
    cat_top = jnp.concatenate([upsample(act_three, depth_mid), skip_input], axis=0)
    ext_top = spatial_halo(cat_top, Z)
    pre_four = conv_forward(ext_top, w_upper, rows_fine, cols_fine, Z)
    features = (
        jax.nn.silu(pre_four).astype(jnp.bfloat16).reshape(top_chan, rows_fine, cols_fine * Z)
    )
    err_four = (cotangent.reshape(top_chan, -1).astype(jnp.float32) * silu_slope(pre_four)).astype(
        jnp.bfloat16
    )
    local_upper = weight_grad(ext_top, err_four, rows_fine, cols_fine, Z) * scale_fine
    grad_upper = lax.psum(local_upper.astype(jnp.bfloat16), ("gx", "gy"))
    dcat_top = conv_backward(
        spatial_halo(err_four.reshape(top_chan, rows_fine, cols_fine * Z), Z),
        w_upper,
        rows_fine,
        cols_fine,
        Z,
    ).reshape(-1, rows_fine, cols_fine * Z)
    mid_chan = act_three.shape[0]
    err_three = (
        block_sum(dcat_top[:mid_chan], Z).reshape(mid_chan, -1) * silu_slope(pre_three)
    ).astype(jnp.bfloat16)
    local_middle = weight_grad(ext_mid, err_three, rows_mid, cols_mid, depth_mid) * scale_mid
    send_middle, grad_upper = lax.optimization_barrier(
        (local_middle.astype(jnp.bfloat16), grad_upper)
    )
    grad_middle = lax.psum(send_middle, ("gx", "gy"))
    dcat_mid = conv_backward(
        spatial_halo(err_three.reshape(mid_chan, rows_mid, cols_mid * depth_mid), depth_mid),
        w_middle,
        rows_mid,
        cols_mid,
        depth_mid,
    ).reshape(-1, rows_mid, cols_mid * depth_mid)
    low_chan = act_two.shape[0]
    dact_two = block_sum(dcat_mid[:low_chan], depth_mid)
    dact_block = lax.all_to_all(dact_two, "gx", split_axis=0, concat_axis=1, tiled=True)
    block_chan = dact_block.shape[0]
    err_two = (dact_block.reshape(block_chan, -1) * silu_slope(pre_two)).astype(jnp.bfloat16)
    part_bottom = weight_grad(ext_low, err_two, rows_all, cols_low, depth_low)
    err_grid = err_two.reshape(block_chan, rows_all, cols_low * depth_low)
    err_cols = extended_2(err_grid, (("gy", 2),), depth_low)
    err_ext = jnp.pad(err_cols, ((0, 0), (1, 1), (0, 0)))
    partial_sum = conv_backward(err_ext, w_bottom, rows_all, cols_low, depth_low).reshape(
        -1, rows_all, cols_low * depth_low
    )
    dpool_parts = lax.all_to_all(
        partial_sum.astype(jnp.bfloat16), "gx", split_axis=1, concat_axis=1, tiled=True
    ).astype(jnp.float32)
    dpool_mid = dpool_parts.reshape(
        dpool_parts.shape[0], lax.axis_size("gx"), rows_low, -1
    ).sum(axis=1)
    send_bottom, grad_middle = lax.optimization_barrier(
        ((part_bottom * scale_low).astype(jnp.bfloat16), grad_middle)
    )
    grad_bottom = lax.psum(send_bottom, "gy")
    dact_one = dcat_mid[low_chan:] + upsample(dpool_mid, depth_low) / 8.0
    err_one = (dact_one.reshape(mid_chan, -1) * silu_slope(pre_one)).astype(jnp.bfloat16)
    local_encoder = weight_grad(ext_pool, err_one, rows_mid, cols_mid, depth_mid) * scale_mid
    send_encoder, grad_bottom = lax.optimization_barrier(
        (local_encoder.astype(jnp.bfloat16), grad_bottom)
    )
    grad_encoder = lax.psum(send_encoder, ("gx", "gy"))
    grad_encoder, grad_bottom, grad_middle, grad_upper = (
        grad.astype(jnp.float32) for grad in (grad_encoder, grad_bottom, grad_middle, grad_upper)
    )
    dpool_top = conv_backward(
        spatial_halo(err_one.reshape(mid_chan, rows_mid, cols_mid * depth_mid), depth_mid),
        w_encoder,
        rows_mid,
        cols_mid,
        depth_mid,
    ).reshape(-1, rows_mid, cols_mid * depth_mid)
    grad_skip = (dcat_top[mid_chan:] + upsample(dpool_top, depth_mid) / 8.0).astype(jnp.bfloat16)
    return (features, grad_skip, grad_encoder, grad_bottom, grad_middle, grad_upper)


def solution(mesh):
    in_specs = (P(None, "gx", "gy"), P(), P("gx", None), P(), P(), P(None, "gx", "gy"))
    out_specs = (P(None, "gx", "gy"), P(None, "gx", "gy"), P(), P("gx", None), P(), P())
    return jax.shard_map(
        per_device, mesh=mesh, in_specs=in_specs, out_specs=out_specs, check_vma=False
    )
```

```python
import functools
import math

import jax
import jax.numpy as jnp
from jax import lax
from jax.experimental import pallas as pl
from jax.experimental.pallas import tpu as pltpu
from jax.sharding import PartitionSpec as P

Z = 16
MESH = pl.DeviceIdType.MESH
VMEM = pl.BlockSpec(memory_space=pltpu.VMEM)
SIDES = ((-1, -1), (-1, 0), (-1, 1), (0, -1), (0, 1), (1, -1), (1, 0), (1, 1))


def halo_kernel(rows_count, cols_count, *refs):
    sent, landed, (send_sem, recv_sem) = refs[:8], refs[8:16], refs[16:]
    row, col = lax.axis_index("gx"), lax.axis_index("gy")
    barrier = pltpu.get_barrier_semaphore()

    def place(side):
        to_row, to_col = row + side[0], col + side[1]
        inside = (to_row >= 0) & (to_row < rows_count) & (to_col >= 0) & (to_col < cols_count)
        return inside, (to_row, to_col)

    for side in SIDES:
        inside, device = place(side)

        @pl.when(inside)
        def _(device=device):
            pl.semaphore_signal(barrier, inc=1, device_id=device, device_id_type=MESH)

    near_rows = 1 + (row > 0).astype(jnp.int32) + (row < rows_count - 1).astype(jnp.int32)
    near_cols = 1 + (col > 0).astype(jnp.int32) + (col < cols_count - 1).astype(jnp.int32)
    pl.semaphore_wait(barrier, near_rows * near_cols - 1)

    def copy(number, device):
        return pltpu.make_async_remote_copy(
            src_ref=sent[number],
            dst_ref=landed[7 - number],
            send_sem=send_sem.at[number],
            recv_sem=recv_sem.at[7 - number],
            device_id=device,
            device_id_type=MESH,
        )

    for number, side in enumerate(SIDES):
        inside, device = place(side)

        @pl.when(inside)
        def _(number=number, device=device):
            copy(number, device).start()

        @pl.when(jnp.logical_not(inside))
        def _(number=number):
            landed[number][...] = jnp.zeros_like(landed[number])

    for number, side in enumerate(SIDES):
        inside, device = place(side)

        @pl.when(inside)
        def _(number=number, device=device):
            copy(number, device).wait_send()
            copy(7 - number, device).wait_recv()


def spatial_halo(cells, width, number):
    channels, rows, length = cells.shape
    strips, shapes = [], []
    for side in SIDES:
        part = cells
        if side[0] != 0:
            part = part[:, :1] if side[0] < 0 else part[:, rows - 1 :]
        if side[1] != 0:
            part = part[:, :, :width] if side[1] < 0 else part[:, :, length - width :]
        shapes.append(part.shape)
        flat = part.reshape(channels, -1)
        strips.append(jnp.pad(flat, ((0, 0), (0, -flat.shape[1] % 128))))
    landed = pl.pallas_call(
        functools.partial(halo_kernel, lax.axis_size("gx"), lax.axis_size("gy")),
        out_shape=[jax.ShapeDtypeStruct(strip.shape, strip.dtype) for strip in strips],
        in_specs=[VMEM] * 8,
        out_specs=[VMEM] * 8,
        scratch_shapes=[pltpu.SemaphoreType.DMA((8,)), pltpu.SemaphoreType.DMA((8,))],
        compiler_params=pltpu.CompilerParams(collective_id=number, has_side_effects=True),
    )(*strips)
    parts = [
        strip[:, : shape[1] * shape[2]].reshape(shape) for strip, shape in zip(landed, shapes)
    ]
    return jnp.concatenate(
        [
            jnp.concatenate(parts[0:3], axis=2),
            jnp.concatenate([parts[3], cells, parts[4]], axis=2),
            jnp.concatenate(parts[5:8], axis=2),
        ],
        axis=1,
    )


def sum_kernel(nx, ny, q, s, big, low, out_big, out_low, first, work, second, result, *sems):
    row, col = lax.axis_index("gx"), lax.axis_index("gy")
    send_one, recv_one, send_two, recv_two, send_three, recv_three, send_four, recv_four = sems
    barrier = pltpu.get_barrier_semaphore()

    def on_row(step):
        return (lax.rem(row + step + nx, nx), col)

    def on_col(step):
        return (row, lax.rem(col + step + ny, ny))

    for step in range(1, nx):
        pl.semaphore_signal(barrier, inc=1, device_id=on_row(step), device_id_type=MESH)
    for step in range(1, ny):
        pl.semaphore_signal(barrier, inc=1, device_id=on_col(step), device_id_type=MESH)
    pl.semaphore_wait(barrier, nx + ny - 2)

    def part(ref, index, width):
        return ref.at[:, pl.ds(pl.multiple_of(index * width, 128), width)]

    def copy(source, target, send, recv, step, device):
        return pltpu.make_async_remote_copy(
            src_ref=source,
            dst_ref=target,
            send_sem=send.at[step],
            recv_sem=recv.at[step],
            device_id=device,
            device_id_type=MESH,
        )

    pending = []
    for step in range(1, nx):
        device = on_row(step)
        pending.append(
            copy(part(big, device[0], q), first.at[step], send_one, recv_one, step, device)
        )
        pending[-1].start()
    width = low.shape[1]
    work[:, pl.ds(q, width)] = low[...]
    if work.shape[1] > q + width:
        rest = work.shape[1] - q - width
        work[:, pl.ds(q + width, rest)] = jnp.zeros((work.shape[0], rest), work.dtype)
    total = part(big, row, q)[...].astype(jnp.float32)
    for step in range(1, nx):
        pending[step - 1].wait_recv()
        total = total + first[step].astype(jnp.float32)
    work[:, pl.ds(0, q)] = total.astype(work.dtype)

    base = len(pending)
    for step in range(1, ny):
        device = on_col(step)
        pending.append(
            copy(part(work, device[1], s), second.at[step], send_two, recv_two, step, device)
        )
        pending[-1].start()
    total = part(work, col, s)[...].astype(jnp.float32)
    for step in range(1, ny):
        pending[base + step - 1].wait_recv()
        total = total + second[step].astype(jnp.float32)
    part(result, col, s)[...] = total.astype(result.dtype)

    for step in range(1, ny):
        device = on_col(step)
        block = part(result, col, s)
        pending.append(copy(block, block, send_three, recv_three, step, device))
        pending[-1].start()
    for step in range(1, ny):
        came = on_col(-step)
        block = part(result, came[1], s)
        copy(block, block, send_three, recv_three, step, came).wait_recv()

    block = result.at[:, pl.ds(0, q)]
    for step in range(1, nx):
        device = on_row(step)
        pending.append(copy(block, part(out_big, row, q), send_four, recv_four, step, device))
        pending[-1].start()
    part(out_big, row, q)[...] = block[...]
    out_low[...] = result[:, pl.ds(q, width)]
    for step in range(1, nx):
        came = on_row(-step)
        copy(block, part(out_big, came[0], q), send_four, recv_four, step, came).wait_recv()
    for sent in pending:
        sent.wait_send()


def folded(grad, rows):
    width = grad.shape[1] * grad.shape[0] // rows
    return jnp.concatenate(
        [grad[:, i * width : (i + 1) * width] for i in range(rows // grad.shape[0])], axis=0
    )


def unfolded(grad, shape):
    count = grad.shape[0] // shape[0]
    return jnp.concatenate(
        [grad[i * shape[0] : (i + 1) * shape[0]] for i in range(count)], axis=1
    ).astype(jnp.float32)


def round_up(value, unit):
    return -(-value // unit) * unit


def summed(grads, low_grad, number):
    nx, ny = lax.axis_size("gx"), lax.axis_size("gy")
    rows = max(grad.shape[0] for grad in grads)
    wide = [folded(grad.astype(jnp.bfloat16), rows) for grad in grads]
    low = folded(low_grad.astype(jnp.bfloat16), rows)
    count = sum(grad.shape[1] for grad in wide)
    q = round_up(round_up(count, nx) // nx, 128)
    width = round_up(low.shape[1], 128)
    s = round_up(round_up(q + width, ny) // ny, 128)
    fill = jnp.zeros((rows, nx * q - count), jnp.bfloat16)
    big = jnp.concatenate(wide + [fill], axis=1)
    low_fill = jnp.pad(low, ((0, 0), (0, width - low.shape[1])))
    out_big, out_low = pl.pallas_call(
        functools.partial(sum_kernel, nx, ny, q, s),
        out_shape=[
            jax.ShapeDtypeStruct(big.shape, big.dtype),
            jax.ShapeDtypeStruct(low_fill.shape, low_fill.dtype),
        ],
        in_specs=[VMEM] * 2,
        out_specs=[VMEM] * 2,
        scratch_shapes=[
            pltpu.VMEM((nx, rows, q), jnp.bfloat16),
            pltpu.VMEM((rows, ny * s), jnp.bfloat16),
            pltpu.VMEM((ny, rows, s), jnp.bfloat16),
            pltpu.VMEM((rows, ny * s), jnp.bfloat16),
        ]
        + [pltpu.SemaphoreType.DMA((count,)) for count in (nx, nx, ny, ny, ny, ny, nx, nx)],
        compiler_params=pltpu.CompilerParams(
            collective_id=number, has_side_effects=True, vmem_limit_bytes=32 << 20
        ),
    )(big, low_fill)
    results, start = [], 0
    for grad, piece in zip(grads, wide):
        results.append(unfolded(out_big[:, start : start + piece.shape[1]], grad.shape))
        start += piece.shape[1]
    return results, unfolded(out_low[:, : low.shape[1]], low_grad.shape)


def extended_2(cells, sides, width):
    for axis, dim in sides:
        count = lax.axis_size(axis)
        ends = count - 1
        head = lax.slice_in_dim(cells, 0, width, axis=dim)
        tail = lax.slice_in_dim(cells, cells.shape[dim] - width, cells.shape[dim], axis=dim)
        cells = jnp.concatenate(
            [
                lax.ppermute(tail, axis, [(i, (i + 1) % count) for i in range(ends)]),
                cells,
                lax.ppermute(head, axis, [((i + 1) % count, i) for i in range(ends)]),
            ],
            axis=dim,
        )
    return cells


def z_shift(extended, z_step, z_depth):
    length = extended.shape[2]
    padded = jnp.pad(extended, ((0, 0), (0, 0), (1, 1)))
    shifted = padded[:, :, 1 + z_step : 1 + z_step + length]
    z_index = lax.broadcasted_iota(jnp.int32, (1, 1, length), 2) % z_depth + z_step
    inside = (z_index >= 0) & (z_index < z_depth)
    return jnp.where(inside, shifted, jnp.zeros_like(shifted))


def tap_piece(shifted_set, a, b, c, row_count, col_count, z_depth, flipped):
    x_off, y_off, z_off = (2 - a, 2 - b, 2 - c) if flipped else (a, b, c)
    source = shifted_set[z_off]
    tap_slice = source[
        :, x_off : x_off + row_count, y_off * z_depth : (y_off + col_count) * z_depth
    ]
    return tap_slice.reshape(source.shape[0], row_count * col_count * z_depth)


def conv_forward(extended, weight, row_count, col_count, z_depth):
    in_chan = extended.shape[0]
    shifted_set = [z_shift(extended, z_step, z_depth) for z_step in (-1, 0, 1)]
    total_sum = jnp.zeros((weight.shape[0], row_count * col_count * z_depth), jnp.float32)
    for a in range(3):
        for b in range(3):
            for c in range(3):
                tap_number = 9 * a + 3 * b + c
                total_sum = total_sum + jnp.dot(
                    weight[:, tap_number * in_chan : (tap_number + 1) * in_chan],
                    tap_piece(shifted_set, a, b, c, row_count, col_count, z_depth, False),
                    preferred_element_type=jnp.float32,
                )
    return total_sum


def conv_backward(extended, weight, row_count, col_count, z_depth):
    in_chan = weight.shape[1] // 27
    shifted_set = [z_shift(extended, z_step, z_depth) for z_step in (-1, 0, 1)]
    total_sum = jnp.zeros((in_chan, row_count * col_count * z_depth), jnp.float32)
    for a in range(3):
        for b in range(3):
            for c in range(3):
                tap_number = 9 * a + 3 * b + c
                total_sum = total_sum + lax.dot_general(
                    weight[:, tap_number * in_chan : (tap_number + 1) * in_chan],
                    tap_piece(shifted_set, a, b, c, row_count, col_count, z_depth, True),
                    (((0,), (0,)), ((), ())),
                    preferred_element_type=jnp.float32,
                )
    return total_sum


def weight_grad(extended, error_flat, row_count, col_count, z_depth):
    shifted_set = [z_shift(extended, z_step, z_depth) for z_step in (-1, 0, 1)]
    blocks = []
    for a in range(3):
        for b in range(3):
            for c in range(3):
                blocks.append(
                    lax.dot_general(
                        error_flat,
                        tap_piece(shifted_set, a, b, c, row_count, col_count, z_depth, False),
                        (((1,), (1,)), ((), ())),
                        preferred_element_type=jnp.float32,
                    )
                )
    return jnp.concatenate(blocks, axis=1)


def pool_mean(values, z_depth):
    channels, row_count, length = values.shape
    col_count = length // z_depth
    shaped = values.astype(jnp.float32).reshape(
        channels, row_count // 2, 2, col_count // 2, 2, z_depth // 2, 2
    )
    return shaped.mean(axis=(2, 4, 6)).reshape(
        channels, row_count // 2, col_count // 2 * (z_depth // 2)
    )


def block_sum(values, z_depth):
    channels, row_count, length = values.shape
    col_count = length // z_depth
    shaped = values.reshape(channels, row_count // 2, 2, col_count // 2, 2, z_depth // 2, 2)
    return shaped.sum(axis=(2, 4, 6)).reshape(
        channels, row_count // 2, col_count // 2 * (z_depth // 2)
    )


def upsample(values, z_depth):
    channels, row_count, length = values.shape
    col_count = length // z_depth
    shaped = values.reshape(channels, row_count, 1, col_count, 1, z_depth, 1)
    shaped = jnp.broadcast_to(shaped, (channels, row_count, 2, col_count, 2, z_depth, 2))
    return shaped.reshape(channels, 2 * row_count, 4 * col_count * z_depth)


def silu_slope(values):
    s_value = jax.nn.sigmoid(values)
    return s_value * (1.0 + values * (1.0 - s_value))


def per_device(skip_input, w_encoder, w_bottom, w_middle, w_upper, cotangent):
    top_chan = skip_input.shape[0]
    rows_fine = skip_input.shape[1]
    cols_fine = skip_input.shape[2] // Z
    rows_mid, cols_mid, depth_mid = (rows_fine // 2, cols_fine // 2, Z // 2)
    rows_low, cols_low, depth_low = (rows_fine // 4, cols_fine // 4, Z // 4)
    cells_fine = rows_fine * cols_fine * Z * lax.axis_size("gx") * lax.axis_size("gy")
    scale_fine = 1.0 / math.sqrt(cells_fine)
    scale_mid = 1.0 / math.sqrt(cells_fine // 8)
    scale_low = 1.0 / math.sqrt(cells_fine // 64)
    pool_top = pool_mean(skip_input, Z).astype(jnp.bfloat16)
    ext_pool = spatial_halo(pool_top, depth_mid, 0)
    pre_one = conv_forward(ext_pool, w_encoder, rows_mid, cols_mid, depth_mid)
    act_one = jax.nn.silu(pre_one).astype(jnp.bfloat16).reshape(-1, rows_mid, cols_mid * depth_mid)
    pool_mid = pool_mean(act_one, depth_mid).astype(jnp.bfloat16)
    col_ext = extended_2(pool_mid, (("gy", 2),), depth_low)
    whole_rows = lax.all_gather(col_ext, "gx", axis=1, tiled=True)
    ext_low = jnp.pad(whole_rows, ((0, 0), (1, 1), (0, 0)))
    rows_all = whole_rows.shape[1]
    pre_two = conv_forward(ext_low, w_bottom, rows_all, cols_low, depth_low)
    act_block = (
        jax.nn.silu(pre_two).astype(jnp.bfloat16).reshape(-1, rows_all, cols_low * depth_low)
    )
    act_two = lax.all_to_all(act_block, "gx", split_axis=1, concat_axis=0, tiled=True)
    cat_mid = jnp.concatenate([upsample(act_two, depth_low), act_one], axis=0)
    ext_mid = spatial_halo(cat_mid, depth_mid, 1)
    pre_three = conv_forward(ext_mid, w_middle, rows_mid, cols_mid, depth_mid)
    act_three = (
        jax.nn.silu(pre_three).astype(jnp.bfloat16).reshape(-1, rows_mid, cols_mid * depth_mid)
    )
    cat_top = jnp.concatenate([upsample(act_three, depth_mid), skip_input], axis=0)
    ext_top = spatial_halo(cat_top, Z, 2)
    pre_four = conv_forward(ext_top, w_upper, rows_fine, cols_fine, Z)
    features = (
        jax.nn.silu(pre_four).astype(jnp.bfloat16).reshape(top_chan, rows_fine, cols_fine * Z)
    )
    err_four = (cotangent.reshape(top_chan, -1).astype(jnp.float32) * silu_slope(pre_four)).astype(
        jnp.bfloat16
    )
    local_upper = weight_grad(ext_top, err_four, rows_fine, cols_fine, Z) * scale_fine
    dcat_top = conv_backward(
        spatial_halo(err_four.reshape(top_chan, rows_fine, cols_fine * Z), Z, 3),
        w_upper,
        rows_fine,
        cols_fine,
        Z,
    ).reshape(-1, rows_fine, cols_fine * Z)
    mid_chan = act_three.shape[0]
    err_three = (
        block_sum(dcat_top[:mid_chan], Z).reshape(mid_chan, -1) * silu_slope(pre_three)
    ).astype(jnp.bfloat16)
    local_middle = weight_grad(ext_mid, err_three, rows_mid, cols_mid, depth_mid) * scale_mid
    dcat_mid = conv_backward(
        spatial_halo(err_three.reshape(mid_chan, rows_mid, cols_mid * depth_mid), depth_mid, 4),
        w_middle,
        rows_mid,
        cols_mid,
        depth_mid,
    ).reshape(-1, rows_mid, cols_mid * depth_mid)
    low_chan = act_two.shape[0]
    dact_two = block_sum(dcat_mid[:low_chan], depth_mid)
    dact_block = lax.all_to_all(dact_two, "gx", split_axis=0, concat_axis=1, tiled=True)
    block_chan = dact_block.shape[0]
    err_two = (dact_block.reshape(block_chan, -1) * silu_slope(pre_two)).astype(jnp.bfloat16)
    part_bottom = weight_grad(ext_low, err_two, rows_all, cols_low, depth_low)
    err_grid = err_two.reshape(block_chan, rows_all, cols_low * depth_low)
    err_cols = extended_2(err_grid, (("gy", 2),), depth_low)
    err_ext = jnp.pad(err_cols, ((0, 0), (1, 1), (0, 0)))
    partial_sum = conv_backward(err_ext, w_bottom, rows_all, cols_low, depth_low).reshape(
        -1, rows_all, cols_low * depth_low
    )
    dpool_parts = lax.all_to_all(
        partial_sum.astype(jnp.bfloat16), "gx", split_axis=1, concat_axis=1, tiled=True
    ).astype(jnp.float32)
    dpool_mid = dpool_parts.reshape(
        dpool_parts.shape[0], lax.axis_size("gx"), rows_low, -1
    ).sum(axis=1)
    dact_one = dcat_mid[low_chan:] + upsample(dpool_mid, depth_low) / 8.0
    err_one = (dact_one.reshape(mid_chan, -1) * silu_slope(pre_one)).astype(jnp.bfloat16)
    local_encoder = weight_grad(ext_pool, err_one, rows_mid, cols_mid, depth_mid) * scale_mid
    (grad_encoder, grad_middle, grad_upper), grad_bottom = summed(
        (local_encoder, local_middle, local_upper), part_bottom * scale_low, 6
    )
    dpool_top = conv_backward(
        spatial_halo(err_one.reshape(mid_chan, rows_mid, cols_mid * depth_mid), depth_mid, 5),
        w_encoder,
        rows_mid,
        cols_mid,
        depth_mid,
    ).reshape(-1, rows_mid, cols_mid * depth_mid)
    grad_skip = (dcat_top[mid_chan:] + upsample(dpool_top, depth_mid) / 8.0).astype(jnp.bfloat16)
    return (features, grad_skip, grad_encoder, grad_bottom, grad_middle, grad_upper)


def solution(mesh):
    in_specs = (P(None, "gx", "gy"), P(), P("gx", None), P(), P(), P(None, "gx", "gy"))
    out_specs = (P(None, "gx", "gy"), P(None, "gx", "gy"), P(), P("gx", None), P(), P())
    return jax.shard_map(
        per_device, mesh=mesh, in_specs=in_specs, out_specs=out_specs, check_vma=False
    )
```

```python
import functools
import math

import jax
import jax.numpy as jnp
from jax import lax
from jax.experimental import pallas as pl
from jax.experimental.pallas import tpu as pltpu
from jax.sharding import PartitionSpec as P

Z = 16
MESH = pl.DeviceIdType.MESH
VMEM = pl.BlockSpec(memory_space=pltpu.VMEM)
SIDES = ((-1, -1), (-1, 0), (-1, 1), (0, -1), (0, 1), (1, -1), (1, 0), (1, 1))


def halo_kernel(rows_count, cols_count, *refs):
    sent, landed, (send_sem, recv_sem) = refs[:8], refs[8:16], refs[16:]
    row, col = lax.axis_index("gx"), lax.axis_index("gy")
    barrier = pltpu.get_barrier_semaphore()

    def place(side):
        to_row, to_col = row + side[0], col + side[1]
        inside = (to_row >= 0) & (to_row < rows_count) & (to_col >= 0) & (to_col < cols_count)
        return inside, (to_row, to_col)

    for side in SIDES:
        inside, device = place(side)

        @pl.when(inside)
        def _(device=device):
            pl.semaphore_signal(barrier, inc=1, device_id=device, device_id_type=MESH)

    near_rows = 1 + (row > 0).astype(jnp.int32) + (row < rows_count - 1).astype(jnp.int32)
    near_cols = 1 + (col > 0).astype(jnp.int32) + (col < cols_count - 1).astype(jnp.int32)
    pl.semaphore_wait(barrier, near_rows * near_cols - 1)

    def copy(number, device):
        return pltpu.make_async_remote_copy(
            src_ref=sent[number],
            dst_ref=landed[7 - number],
            send_sem=send_sem.at[number],
            recv_sem=recv_sem.at[7 - number],
            device_id=device,
            device_id_type=MESH,
        )

    for number, side in enumerate(SIDES):
        inside, device = place(side)

        @pl.when(inside)
        def _(number=number, device=device):
            copy(number, device).start()

        @pl.when(jnp.logical_not(inside))
        def _(number=number):
            landed[number][...] = jnp.zeros_like(landed[number])

    for number, side in enumerate(SIDES):
        inside, device = place(side)

        @pl.when(inside)
        def _(number=number, device=device):
            copy(number, device).wait_send()
            copy(7 - number, device).wait_recv()


def spatial_halo(cells, width, number):
    channels, rows, length = cells.shape
    strips, shapes = [], []
    for side in SIDES:
        part = cells
        if side[0] != 0:
            part = part[:, :1] if side[0] < 0 else part[:, rows - 1 :]
        if side[1] != 0:
            part = part[:, :, :width] if side[1] < 0 else part[:, :, length - width :]
        shapes.append(part.shape)
        flat = part.reshape(channels, -1)
        strips.append(jnp.pad(flat, ((0, 0), (0, -flat.shape[1] % 128))))
    landed = pl.pallas_call(
        functools.partial(halo_kernel, lax.axis_size("gx"), lax.axis_size("gy")),
        out_shape=[jax.ShapeDtypeStruct(strip.shape, strip.dtype) for strip in strips],
        in_specs=[VMEM] * 8,
        out_specs=[VMEM] * 8,
        scratch_shapes=[pltpu.SemaphoreType.DMA((8,)), pltpu.SemaphoreType.DMA((8,))],
        compiler_params=pltpu.CompilerParams(collective_id=number, has_side_effects=True),
    )(*strips)
    parts = [
        strip[:, : shape[1] * shape[2]].reshape(shape) for strip, shape in zip(landed, shapes)
    ]
    return jnp.concatenate(
        [
            jnp.concatenate(parts[0:3], axis=2),
            jnp.concatenate([parts[3], cells, parts[4]], axis=2),
            jnp.concatenate(parts[5:8], axis=2),
        ],
        axis=1,
    )


def sum_kernel(nx, ny, q, s, big, low, out_big, out_low, first, work, second, result, *sems):
    row, col = lax.axis_index("gx"), lax.axis_index("gy")
    send_one, recv_one, send_two, recv_two, send_three, recv_three, send_four, recv_four = sems
    barrier = pltpu.get_barrier_semaphore()

    def on_row(step):
        return (lax.rem(row + step + nx, nx), col)

    def on_col(step):
        return (row, lax.rem(col + step + ny, ny))

    for step in range(1, nx):
        pl.semaphore_signal(barrier, inc=1, device_id=on_row(step), device_id_type=MESH)
    for step in range(1, ny):
        pl.semaphore_signal(barrier, inc=1, device_id=on_col(step), device_id_type=MESH)
    pl.semaphore_wait(barrier, nx + ny - 2)

    def part(ref, index, width):
        return ref.at[:, pl.ds(pl.multiple_of(index * width, 128), width)]

    def copy(source, target, send, recv, step, device):
        return pltpu.make_async_remote_copy(
            src_ref=source,
            dst_ref=target,
            send_sem=send.at[step],
            recv_sem=recv.at[step],
            device_id=device,
            device_id_type=MESH,
        )

    pending = []
    for step in range(1, nx):
        device = on_row(step)
        pending.append(
            copy(part(big, device[0], q), first.at[step], send_one, recv_one, step, device)
        )
        pending[-1].start()
    width = low.shape[1]
    work[:, pl.ds(q, width)] = low[...]
    if work.shape[1] > q + width:
        rest = work.shape[1] - q - width
        work[:, pl.ds(q + width, rest)] = jnp.zeros((work.shape[0], rest), work.dtype)
    total = part(big, row, q)[...].astype(jnp.float32)
    for step in range(1, nx):
        pending[step - 1].wait_recv()
        total = total + first[step].astype(jnp.float32)
    work[:, pl.ds(0, q)] = total.astype(work.dtype)

    base = len(pending)
    for step in range(1, ny):
        device = on_col(step)
        pending.append(
            copy(part(work, device[1], s), second.at[step], send_two, recv_two, step, device)
        )
        pending[-1].start()
    total = part(work, col, s)[...].astype(jnp.float32)
    for step in range(1, ny):
        pending[base + step - 1].wait_recv()
        total = total + second[step].astype(jnp.float32)
    part(result, col, s)[...] = total.astype(result.dtype)

    for step in range(1, ny):
        device = on_col(step)
        block = part(result, col, s)
        pending.append(copy(block, block, send_three, recv_three, step, device))
        pending[-1].start()
    for step in range(1, ny):
        came = on_col(-step)
        block = part(result, came[1], s)
        copy(block, block, send_three, recv_three, step, came).wait_recv()

    block = result.at[:, pl.ds(0, q)]
    for step in range(1, nx):
        device = on_row(step)
        pending.append(copy(block, part(out_big, row, q), send_four, recv_four, step, device))
        pending[-1].start()
    part(out_big, row, q)[...] = block[...]
    out_low[...] = result[:, pl.ds(q, width)]
    for step in range(1, nx):
        came = on_row(-step)
        copy(block, part(out_big, came[0], q), send_four, recv_four, step, came).wait_recv()
    for sent in pending:
        sent.wait_send()


def folded(grad, rows):
    width = grad.shape[1] * grad.shape[0] // rows
    return jnp.concatenate(
        [grad[:, i * width : (i + 1) * width] for i in range(rows // grad.shape[0])], axis=0
    )


def unfolded(grad, shape):
    count = grad.shape[0] // shape[0]
    return jnp.concatenate(
        [grad[i * shape[0] : (i + 1) * shape[0]] for i in range(count)], axis=1
    ).astype(jnp.float32)


def round_up(value, unit):
    return -(-value // unit) * unit


def summed(grads, low_grad, number):
    nx, ny = lax.axis_size("gx"), lax.axis_size("gy")
    rows = max(grad.shape[0] for grad in grads)
    wide = [folded(grad.astype(jnp.bfloat16), rows) for grad in grads]
    low = folded(low_grad.astype(jnp.bfloat16), rows)
    count = sum(grad.shape[1] for grad in wide)
    q = round_up(round_up(count, nx) // nx, 128)
    width = round_up(low.shape[1], 128)
    s = round_up(round_up(q + width, ny) // ny, 128)
    fill = jnp.zeros((rows, nx * q - count), jnp.bfloat16)
    big = jnp.concatenate(wide + [fill], axis=1)
    low_fill = jnp.pad(low, ((0, 0), (0, width - low.shape[1])))
    out_big, out_low = pl.pallas_call(
        functools.partial(sum_kernel, nx, ny, q, s),
        out_shape=[
            jax.ShapeDtypeStruct(big.shape, big.dtype),
            jax.ShapeDtypeStruct(low_fill.shape, low_fill.dtype),
        ],
        in_specs=[VMEM] * 2,
        out_specs=[VMEM] * 2,
        scratch_shapes=[
            pltpu.VMEM((nx, rows, q), jnp.bfloat16),
            pltpu.VMEM((rows, ny * s), jnp.bfloat16),
            pltpu.VMEM((ny, rows, s), jnp.bfloat16),
            pltpu.VMEM((rows, ny * s), jnp.bfloat16),
        ]
        + [pltpu.SemaphoreType.DMA((count,)) for count in (nx, nx, ny, ny, ny, ny, nx, nx)],
        compiler_params=pltpu.CompilerParams(
            collective_id=number, has_side_effects=True, vmem_limit_bytes=32 << 20
        ),
    )(big, low_fill)
    results, start = [], 0
    for grad, piece in zip(grads, wide):
        results.append(unfolded(out_big[:, start : start + piece.shape[1]], grad.shape))
        start += piece.shape[1]
    return results, unfolded(out_low[:, : low.shape[1]], low_grad.shape)


def extended_2(cells, sides, width):
    for axis, dim in sides:
        count = lax.axis_size(axis)
        ends = count - 1
        head = lax.slice_in_dim(cells, 0, width, axis=dim)
        tail = lax.slice_in_dim(cells, cells.shape[dim] - width, cells.shape[dim], axis=dim)
        cells = jnp.concatenate(
            [
                lax.ppermute(tail, axis, [(i, (i + 1) % count) for i in range(ends)]),
                cells,
                lax.ppermute(head, axis, [((i + 1) % count, i) for i in range(ends)]),
            ],
            axis=dim,
        )
    return cells


def stack_taps(x_ref, stack, z_depth):
    channels, length = x_ref.shape
    values = x_ref[...].astype(jnp.float32)
    z_index = lax.broadcasted_iota(jnp.int32, (channels, length), 1) % z_depth
    for b in range(3):
        for c in range(3):
            moved = pltpu.roll(values, (length - b * z_depth - c + 1) % length, 1)
            if c != 1:
                moved = jnp.where(z_index != (0 if c == 0 else z_depth - 1), moved, 0.0)
            tap = 3 * b + c
            stack[tap * channels : (tap + 1) * channels, :] = moved.astype(jnp.bfloat16)
    if stack.shape[0] > 9 * channels:
        rest = stack.shape[0] - 9 * channels
        stack[9 * channels :, :] = jnp.zeros((rest, length), jnp.bfloat16)


def conv_kernel(z_depth, row_count, x_ref, w_ref, out_ref, stack):
    stack_taps(x_ref, stack, z_depth)
    length = x_ref.shape[1] // (row_count + 2)
    total = jnp.dot(w_ref[...], stack[...], preferred_element_type=jnp.float32)
    chan = out_ref.shape[0]
    out_ref[...] = sum(
        total[a * chan : (a + 1) * chan, a * length : (a + row_count) * length] for a in range(3)
    )


def grad_kernel(z_depth, row_count, x_ref, error_ref, out_ref, stack):
    stack_taps(x_ref, stack, z_depth)
    length = x_ref.shape[1] // (row_count + 2)
    for a in range(3):
        out_ref[a] = lax.dot_general(
            error_ref[...],
            stack[:, a * length : (a + row_count) * length],
            (((1,), (1,)), ((), ())),
            preferred_element_type=jnp.float32,
        )


def widened(values, length):
    padded = jnp.pad(values, ((0, 0), (0, 0), (0, length - values.shape[2])))
    return padded.reshape(values.shape[0], -1)


def local_call(kernel, extended, other, out_shape, row_count, z_depth):
    length = round_up(extended.shape[2], 128)
    flat = widened(extended, length)
    depth = round_up(9 * flat.shape[0], 128)
    return pl.pallas_call(
        functools.partial(kernel, z_depth, row_count),
        out_shape=jax.ShapeDtypeStruct(out_shape, jnp.float32),
        in_specs=[VMEM] * 2,
        out_specs=VMEM,
        scratch_shapes=[pltpu.VMEM((depth, flat.shape[1]), jnp.bfloat16)],
        compiler_params=pltpu.CompilerParams(vmem_limit_bytes=40 << 20),
    )(flat, other)


def conv_local(extended, taps, out_chan, row_count, col_count, z_depth):
    length = round_up(extended.shape[2], 128)
    weight = taps.reshape(3 * out_chan, -1)
    weight = jnp.pad(weight, ((0, 0), (0, -weight.shape[1] % 128)))
    out = local_call(
        conv_kernel, extended, weight, (out_chan, row_count * length), row_count, z_depth
    )
    out = out.reshape(out_chan, row_count, length)[:, :, : col_count * z_depth]
    return out.reshape(out_chan, -1)


def conv_forward(extended, weight, row_count, col_count, z_depth):
    out_chan = weight.shape[0]
    taps = weight.reshape(out_chan, 3, -1).transpose(1, 0, 2)
    return conv_local(extended, taps, out_chan, row_count, col_count, z_depth)


def conv_backward(extended, weight, row_count, col_count, z_depth):
    out_chan, in_chan = weight.shape[0], weight.shape[1] // 27
    taps = weight.reshape(out_chan, 27, in_chan)[:, ::-1].transpose(1, 2, 0)
    taps = taps.reshape(3, 9, in_chan, out_chan).transpose(0, 2, 1, 3)
    return conv_local(extended, taps, in_chan, row_count, col_count, z_depth)


def weight_grad(extended, error_flat, row_count, col_count, z_depth):
    in_chan, out_chan = extended.shape[0], error_flat.shape[0]
    error = widened(
        error_flat.reshape(out_chan, row_count, -1), round_up(extended.shape[2], 128)
    )
    shape = (3, out_chan, round_up(9 * in_chan, 128))
    out = local_call(grad_kernel, extended, error, shape, row_count, z_depth)
    return jnp.concatenate([out[a, :, : 9 * in_chan] for a in range(3)], axis=1)


def pool_mean(values, z_depth):
    channels, row_count, length = values.shape
    col_count = length // z_depth
    shaped = values.astype(jnp.float32).reshape(
        channels, row_count // 2, 2, col_count // 2, 2, z_depth // 2, 2
    )
    return shaped.mean(axis=(2, 4, 6)).reshape(
        channels, row_count // 2, col_count // 2 * (z_depth // 2)
    )


def block_sum(values, z_depth):
    channels, row_count, length = values.shape
    col_count = length // z_depth
    shaped = values.reshape(channels, row_count // 2, 2, col_count // 2, 2, z_depth // 2, 2)
    return shaped.sum(axis=(2, 4, 6)).reshape(
        channels, row_count // 2, col_count // 2 * (z_depth // 2)
    )


def upsample(values, z_depth):
    channels, row_count, length = values.shape
    col_count = length // z_depth
    shaped = values.reshape(channels, row_count, 1, col_count, 1, z_depth, 1)
    shaped = jnp.broadcast_to(shaped, (channels, row_count, 2, col_count, 2, z_depth, 2))
    return shaped.reshape(channels, 2 * row_count, 4 * col_count * z_depth)


def silu_slope(values):
    s_value = jax.nn.sigmoid(values)
    return s_value * (1.0 + values * (1.0 - s_value))


def per_device(skip_input, w_encoder, w_bottom, w_middle, w_upper, cotangent):
    top_chan = skip_input.shape[0]
    rows_fine = skip_input.shape[1]
    cols_fine = skip_input.shape[2] // Z
    rows_mid, cols_mid, depth_mid = (rows_fine // 2, cols_fine // 2, Z // 2)
    rows_low, cols_low, depth_low = (rows_fine // 4, cols_fine // 4, Z // 4)
    cells_fine = rows_fine * cols_fine * Z * lax.axis_size("gx") * lax.axis_size("gy")
    scale_fine = 1.0 / math.sqrt(cells_fine)
    scale_mid = 1.0 / math.sqrt(cells_fine // 8)
    scale_low = 1.0 / math.sqrt(cells_fine // 64)
    pool_top = pool_mean(skip_input, Z).astype(jnp.bfloat16)
    ext_pool = spatial_halo(pool_top, depth_mid, 0)
    pre_one = conv_forward(ext_pool, w_encoder, rows_mid, cols_mid, depth_mid)
    act_one = jax.nn.silu(pre_one).astype(jnp.bfloat16).reshape(-1, rows_mid, cols_mid * depth_mid)
    pool_mid = pool_mean(act_one, depth_mid).astype(jnp.bfloat16)
    col_ext = extended_2(pool_mid, (("gy", 2),), depth_low)
    whole_rows = lax.all_gather(col_ext, "gx", axis=1, tiled=True)
    ext_low = jnp.pad(whole_rows, ((0, 0), (1, 1), (0, 0)))
    rows_all = whole_rows.shape[1]
    pre_two = conv_forward(ext_low, w_bottom, rows_all, cols_low, depth_low)
    act_block = (
        jax.nn.silu(pre_two).astype(jnp.bfloat16).reshape(-1, rows_all, cols_low * depth_low)
    )
    act_two = lax.all_to_all(act_block, "gx", split_axis=1, concat_axis=0, tiled=True)
    cat_mid = jnp.concatenate([upsample(act_two, depth_low), act_one], axis=0)
    ext_mid = spatial_halo(cat_mid, depth_mid, 1)
    pre_three = conv_forward(ext_mid, w_middle, rows_mid, cols_mid, depth_mid)
    act_three = (
        jax.nn.silu(pre_three).astype(jnp.bfloat16).reshape(-1, rows_mid, cols_mid * depth_mid)
    )
    cat_top = jnp.concatenate([upsample(act_three, depth_mid), skip_input], axis=0)
    ext_top = spatial_halo(cat_top, Z, 2)
    pre_four = conv_forward(ext_top, w_upper, rows_fine, cols_fine, Z)
    features = (
        jax.nn.silu(pre_four).astype(jnp.bfloat16).reshape(top_chan, rows_fine, cols_fine * Z)
    )
    err_four = (cotangent.reshape(top_chan, -1).astype(jnp.float32) * silu_slope(pre_four)).astype(
        jnp.bfloat16
    )
    local_upper = weight_grad(ext_top, err_four, rows_fine, cols_fine, Z) * scale_fine
    dcat_top = conv_backward(
        spatial_halo(err_four.reshape(top_chan, rows_fine, cols_fine * Z), Z, 3),
        w_upper,
        rows_fine,
        cols_fine,
        Z,
    ).reshape(-1, rows_fine, cols_fine * Z)
    mid_chan = act_three.shape[0]
    err_three = (
        block_sum(dcat_top[:mid_chan], Z).reshape(mid_chan, -1) * silu_slope(pre_three)
    ).astype(jnp.bfloat16)
    local_middle = weight_grad(ext_mid, err_three, rows_mid, cols_mid, depth_mid) * scale_mid
    dcat_mid = conv_backward(
        spatial_halo(err_three.reshape(mid_chan, rows_mid, cols_mid * depth_mid), depth_mid, 4),
        w_middle,
        rows_mid,
        cols_mid,
        depth_mid,
    ).reshape(-1, rows_mid, cols_mid * depth_mid)
    low_chan = act_two.shape[0]
    dact_two = block_sum(dcat_mid[:low_chan], depth_mid)
    dact_block = lax.all_to_all(dact_two, "gx", split_axis=0, concat_axis=1, tiled=True)
    block_chan = dact_block.shape[0]
    err_two = (dact_block.reshape(block_chan, -1) * silu_slope(pre_two)).astype(jnp.bfloat16)
    part_bottom = weight_grad(ext_low, err_two, rows_all, cols_low, depth_low)
    err_grid = err_two.reshape(block_chan, rows_all, cols_low * depth_low)
    err_cols = extended_2(err_grid, (("gy", 2),), depth_low)
    err_ext = jnp.pad(err_cols, ((0, 0), (1, 1), (0, 0)))
    partial_sum = conv_backward(err_ext, w_bottom, rows_all, cols_low, depth_low).reshape(
        -1, rows_all, cols_low * depth_low
    )
    dpool_parts = lax.all_to_all(
        partial_sum.astype(jnp.bfloat16), "gx", split_axis=1, concat_axis=1, tiled=True
    ).astype(jnp.float32)
    dpool_mid = dpool_parts.reshape(
        dpool_parts.shape[0], lax.axis_size("gx"), rows_low, -1
    ).sum(axis=1)
    dact_one = dcat_mid[low_chan:] + upsample(dpool_mid, depth_low) / 8.0
    err_one = (dact_one.reshape(mid_chan, -1) * silu_slope(pre_one)).astype(jnp.bfloat16)
    local_encoder = weight_grad(ext_pool, err_one, rows_mid, cols_mid, depth_mid) * scale_mid
    (grad_encoder, grad_middle, grad_upper), grad_bottom = summed(
        (local_encoder, local_middle, local_upper), part_bottom * scale_low, 6
    )
    dpool_top = conv_backward(
        spatial_halo(err_one.reshape(mid_chan, rows_mid, cols_mid * depth_mid), depth_mid, 5),
        w_encoder,
        rows_mid,
        cols_mid,
        depth_mid,
    ).reshape(-1, rows_mid, cols_mid * depth_mid)
    grad_skip = (dcat_top[mid_chan:] + upsample(dpool_top, depth_mid) / 8.0).astype(jnp.bfloat16)
    return (features, grad_skip, grad_encoder, grad_bottom, grad_middle, grad_upper)


def solution(mesh):
    in_specs = (P(None, "gx", "gy"), P(), P("gx", None), P(), P(), P(None, "gx", "gy"))
    out_specs = (P(None, "gx", "gy"), P(None, "gx", "gy"), P(), P("gx", None), P(), P())
    return jax.shard_map(
        per_device, mesh=mesh, in_specs=in_specs, out_specs=out_specs, check_vma=False
    )
```

```python
import functools
import math

import jax
import jax.numpy as jnp
from jax import lax
from jax.experimental import pallas as pl
from jax.experimental.pallas import tpu as pltpu
from jax.sharding import PartitionSpec as P

Z = 16
MESH = pl.DeviceIdType.MESH
VMEM = pl.BlockSpec(memory_space=pltpu.VMEM)
SIDES = ((-1, -1), (-1, 0), (-1, 1), (0, -1), (0, 1), (1, -1), (1, 0), (1, 1))


def halo_kernel(rows_count, cols_count, *refs):
    sent, landed, (send_sem, recv_sem) = refs[:8], refs[8:16], refs[16:]
    row, col = lax.axis_index("gx"), lax.axis_index("gy")
    barrier = pltpu.get_barrier_semaphore()

    def place(side):
        to_row, to_col = row + side[0], col + side[1]
        inside = (to_row >= 0) & (to_row < rows_count) & (to_col >= 0) & (to_col < cols_count)
        return inside, (to_row, to_col)

    for side in SIDES:
        inside, device = place(side)

        @pl.when(inside)
        def _(device=device):
            pl.semaphore_signal(barrier, inc=1, device_id=device, device_id_type=MESH)

    near_rows = 1 + (row > 0).astype(jnp.int32) + (row < rows_count - 1).astype(jnp.int32)
    near_cols = 1 + (col > 0).astype(jnp.int32) + (col < cols_count - 1).astype(jnp.int32)
    pl.semaphore_wait(barrier, near_rows * near_cols - 1)

    def copy(number, device):
        return pltpu.make_async_remote_copy(
            src_ref=sent[number],
            dst_ref=landed[7 - number],
            send_sem=send_sem.at[number],
            recv_sem=recv_sem.at[7 - number],
            device_id=device,
            device_id_type=MESH,
        )

    for number, side in enumerate(SIDES):
        inside, device = place(side)

        @pl.when(inside)
        def _(number=number, device=device):
            copy(number, device).start()

        @pl.when(jnp.logical_not(inside))
        def _(number=number):
            landed[number][...] = jnp.zeros_like(landed[number])

    for number, side in enumerate(SIDES):
        inside, device = place(side)

        @pl.when(inside)
        def _(number=number, device=device):
            copy(number, device).wait_send()
            copy(7 - number, device).wait_recv()


def spatial_halo(cells, width, number):
    channels, rows, length = cells.shape
    strips, shapes = [], []
    for side in SIDES:
        part = cells
        if side[0] != 0:
            part = part[:, :1] if side[0] < 0 else part[:, rows - 1 :]
        if side[1] != 0:
            part = part[:, :, :width] if side[1] < 0 else part[:, :, length - width :]
        shapes.append(part.shape)
        strips.append(part.reshape(channels, -1))
    landed = pl.pallas_call(
        functools.partial(halo_kernel, lax.axis_size("gx"), lax.axis_size("gy")),
        out_shape=[jax.ShapeDtypeStruct(strip.shape, strip.dtype) for strip in strips],
        in_specs=[VMEM] * 8,
        out_specs=[VMEM] * 8,
        scratch_shapes=[pltpu.SemaphoreType.DMA((8,)), pltpu.SemaphoreType.DMA((8,))],
        compiler_params=pltpu.CompilerParams(collective_id=number, has_side_effects=True),
    )(*strips)
    parts = [strip.reshape(shape) for strip, shape in zip(landed, shapes)]
    return jnp.concatenate(
        [
            jnp.concatenate(parts[0:3], axis=2),
            jnp.concatenate([parts[3], cells, parts[4]], axis=2),
            jnp.concatenate(parts[5:8], axis=2),
        ],
        axis=1,
    )


def sum_kernel(nx, ny, q, s, big, low, out_big, out_low, first, work, second, result, *sems):
    row, col = lax.axis_index("gx"), lax.axis_index("gy")
    send_one, recv_one, send_two, recv_two, send_three, recv_three, send_four, recv_four = sems
    barrier = pltpu.get_barrier_semaphore()

    def on_row(step):
        return (lax.rem(row + step + nx, nx), col)

    def on_col(step):
        return (row, lax.rem(col + step + ny, ny))

    for step in range(1, nx):
        pl.semaphore_signal(barrier, inc=1, device_id=on_row(step), device_id_type=MESH)
    for step in range(1, ny):
        pl.semaphore_signal(barrier, inc=1, device_id=on_col(step), device_id_type=MESH)
    pl.semaphore_wait(barrier, nx + ny - 2)

    def part(ref, index, width):
        return ref.at[:, pl.ds(pl.multiple_of(index * width, 128), width)]

    def copy(source, target, send, recv, step, device):
        return pltpu.make_async_remote_copy(
            src_ref=source,
            dst_ref=target,
            send_sem=send.at[step],
            recv_sem=recv.at[step],
            device_id=device,
            device_id_type=MESH,
        )

    pending = []
    for step in range(1, nx):
        device = on_row(step)
        pending.append(
            copy(part(big, device[0], q), first.at[step], send_one, recv_one, step, device)
        )
        pending[-1].start()
    width = low.shape[1]
    work[:, pl.ds(q, width)] = low[...]
    if work.shape[1] > q + width:
        rest = work.shape[1] - q - width
        work[:, pl.ds(q + width, rest)] = jnp.zeros((work.shape[0], rest), work.dtype)
    total = part(big, row, q)[...].astype(jnp.float32)
    for step in range(1, nx):
        pending[step - 1].wait_recv()
        total = total + first[step].astype(jnp.float32)
    work[:, pl.ds(0, q)] = total.astype(work.dtype)

    base = len(pending)
    for step in range(1, ny):
        device = on_col(step)
        pending.append(
            copy(part(work, device[1], s), second.at[step], send_two, recv_two, step, device)
        )
        pending[-1].start()
    total = part(work, col, s)[...].astype(jnp.float32)
    for step in range(1, ny):
        pending[base + step - 1].wait_recv()
        total = total + second[step].astype(jnp.float32)
    part(result, col, s)[...] = total.astype(result.dtype)

    for step in range(1, ny):
        device = on_col(step)
        block = part(result, col, s)
        pending.append(copy(block, block, send_three, recv_three, step, device))
        pending[-1].start()
    for step in range(1, ny):
        came = on_col(-step)
        block = part(result, came[1], s)
        copy(block, block, send_three, recv_three, step, came).wait_recv()

    block = result.at[:, pl.ds(0, q)]
    for step in range(1, nx):
        device = on_row(step)
        pending.append(copy(block, part(out_big, row, q), send_four, recv_four, step, device))
        pending[-1].start()
    part(out_big, row, q)[...] = block[...]
    out_low[...] = result[:, pl.ds(q, width)]
    for step in range(1, nx):
        came = on_row(-step)
        copy(block, part(out_big, came[0], q), send_four, recv_four, step, came).wait_recv()
    for sent in pending:
        sent.wait_send()


def folded(grad, rows):
    width = grad.shape[1] * grad.shape[0] // rows
    return jnp.concatenate(
        [grad[:, i * width : (i + 1) * width] for i in range(rows // grad.shape[0])], axis=0
    )


def unfolded(grad, shape):
    count = grad.shape[0] // shape[0]
    return jnp.concatenate(
        [grad[i * shape[0] : (i + 1) * shape[0]] for i in range(count)], axis=1
    ).astype(jnp.float32)


def round_up(value, unit):
    return -(-value // unit) * unit


def summed(grads, low_grad, number):
    nx, ny = lax.axis_size("gx"), lax.axis_size("gy")
    rows = max(grad.shape[0] for grad in grads)
    wide = [folded(grad.astype(jnp.bfloat16), rows) for grad in grads]
    low = folded(low_grad.astype(jnp.bfloat16), rows)
    count = sum(grad.shape[1] for grad in wide)
    q = round_up(round_up(count, nx) // nx, 128)
    width = round_up(low.shape[1], 128)
    s = round_up(round_up(q + width, ny) // ny, 128)
    fill = jnp.zeros((rows, nx * q - count), jnp.bfloat16)
    big = jnp.concatenate(wide + [fill], axis=1)
    low_fill = jnp.pad(low, ((0, 0), (0, width - low.shape[1])))
    out_big, out_low = pl.pallas_call(
        functools.partial(sum_kernel, nx, ny, q, s),
        out_shape=[
            jax.ShapeDtypeStruct(big.shape, big.dtype),
            jax.ShapeDtypeStruct(low_fill.shape, low_fill.dtype),
        ],
        in_specs=[VMEM] * 2,
        out_specs=[VMEM] * 2,
        scratch_shapes=[
            pltpu.VMEM((nx, rows, q), jnp.bfloat16),
            pltpu.VMEM((rows, ny * s), jnp.bfloat16),
            pltpu.VMEM((ny, rows, s), jnp.bfloat16),
            pltpu.VMEM((rows, ny * s), jnp.bfloat16),
        ]
        + [pltpu.SemaphoreType.DMA((count,)) for count in (nx, nx, ny, ny, ny, ny, nx, nx)],
        compiler_params=pltpu.CompilerParams(
            collective_id=number, has_side_effects=True, vmem_limit_bytes=32 << 20
        ),
    )(big, low_fill)
    results, start = [], 0
    for grad, piece in zip(grads, wide):
        results.append(unfolded(out_big[:, start : start + piece.shape[1]], grad.shape))
        start += piece.shape[1]
    return results, unfolded(out_low[:, : low.shape[1]], low_grad.shape)


def extended_2(cells, sides, width):
    for axis, dim in sides:
        count = lax.axis_size(axis)
        ends = count - 1
        head = lax.slice_in_dim(cells, 0, width, axis=dim)
        tail = lax.slice_in_dim(cells, cells.shape[dim] - width, cells.shape[dim], axis=dim)
        cells = jnp.concatenate(
            [
                lax.ppermute(tail, axis, [(i, (i + 1) % count) for i in range(ends)]),
                cells,
                lax.ppermute(head, axis, [((i + 1) % count, i) for i in range(ends)]),
            ],
            axis=dim,
        )
    return cells


def stack_taps(x_ref, stack, z_depth):
    channels, length = x_ref.shape
    values = x_ref[...].astype(jnp.float32)
    z_index = lax.broadcasted_iota(jnp.int32, (channels, length), 1) % z_depth
    for b in range(3):
        for c in range(3):
            moved = pltpu.roll(values, (length - b * z_depth - c + 1) % length, 1)
            if c != 1:
                moved = jnp.where(z_index != (0 if c == 0 else z_depth - 1), moved, 0.0)
            tap = 3 * b + c
            stack[tap * channels : (tap + 1) * channels, :] = moved.astype(jnp.bfloat16)
    if stack.shape[0] > 9 * channels:
        rest = stack.shape[0] - 9 * channels
        stack[9 * channels :, :] = jnp.zeros((rest, length), jnp.bfloat16)


def conv_kernel(z_depth, row_count, x_ref, w_ref, out_ref, stack):
    stack_taps(x_ref, stack, z_depth)
    length = x_ref.shape[1] // (row_count + 2)
    total = jnp.dot(w_ref[...], stack[...], preferred_element_type=jnp.float32)
    chan = out_ref.shape[0]
    out_ref[...] = sum(
        total[a * chan : (a + 1) * chan, a * length : (a + row_count) * length] for a in range(3)
    )


def grad_kernel(z_depth, row_count, x_ref, error_ref, out_ref, stack):
    stack_taps(x_ref, stack, z_depth)
    length = x_ref.shape[1] // (row_count + 2)
    for a in range(3):
        out_ref[a] = lax.dot_general(
            error_ref[...],
            stack[:, a * length : (a + row_count) * length],
            (((1,), (1,)), ((), ())),
            preferred_element_type=jnp.float32,
        )


def widened(values, length):
    padded = jnp.pad(values, ((0, 0), (0, 0), (0, length - values.shape[2])))
    return padded.reshape(values.shape[0], -1)


def local_call(kernel, extended, other, out_shape, row_count, z_depth):
    length = round_up(extended.shape[2], 128)
    flat = widened(extended, length)
    depth = round_up(9 * flat.shape[0], 128)
    return pl.pallas_call(
        functools.partial(kernel, z_depth, row_count),
        out_shape=jax.ShapeDtypeStruct(out_shape, jnp.float32),
        in_specs=[VMEM] * 2,
        out_specs=VMEM,
        scratch_shapes=[pltpu.VMEM((depth, flat.shape[1]), jnp.bfloat16)],
        compiler_params=pltpu.CompilerParams(vmem_limit_bytes=40 << 20),
    )(flat, other)


def conv_local(extended, taps, out_chan, row_count, col_count, z_depth):
    length = round_up(extended.shape[2], 128)
    weight = taps.reshape(3 * out_chan, -1)
    weight = jnp.pad(weight, ((0, 0), (0, -weight.shape[1] % 128)))
    out = local_call(
        conv_kernel, extended, weight, (out_chan, row_count * length), row_count, z_depth
    )
    out = out.reshape(out_chan, row_count, length)[:, :, : col_count * z_depth]
    return out.reshape(out_chan, -1)


def conv_forward(extended, weight, row_count, col_count, z_depth):
    out_chan = weight.shape[0]
    taps = weight.reshape(out_chan, 3, -1).transpose(1, 0, 2)
    return conv_local(extended, taps, out_chan, row_count, col_count, z_depth)


def conv_backward(extended, weight, row_count, col_count, z_depth):
    out_chan, in_chan = weight.shape[0], weight.shape[1] // 27
    taps = weight.reshape(out_chan, 27, in_chan)[:, ::-1].transpose(1, 2, 0)
    taps = taps.reshape(3, 9, in_chan, out_chan).transpose(0, 2, 1, 3)
    return conv_local(extended, taps, in_chan, row_count, col_count, z_depth)


def weight_grad(extended, error_flat, row_count, col_count, z_depth):
    in_chan, out_chan = extended.shape[0], error_flat.shape[0]
    error = widened(
        error_flat.reshape(out_chan, row_count, -1), round_up(extended.shape[2], 128)
    )
    shape = (3, out_chan, round_up(9 * in_chan, 128))
    out = local_call(grad_kernel, extended, error, shape, row_count, z_depth)
    return jnp.concatenate([out[a, :, : 9 * in_chan] for a in range(3)], axis=1)


def pool_mean(values, z_depth):
    channels, row_count, length = values.shape
    col_count = length // z_depth
    shaped = values.astype(jnp.float32).reshape(
        channels, row_count // 2, 2, col_count // 2, 2, z_depth // 2, 2
    )
    return shaped.mean(axis=(2, 4, 6)).reshape(
        channels, row_count // 2, col_count // 2 * (z_depth // 2)
    )


def block_sum(values, z_depth):
    channels, row_count, length = values.shape
    col_count = length // z_depth
    shaped = values.reshape(channels, row_count // 2, 2, col_count // 2, 2, z_depth // 2, 2)
    return shaped.sum(axis=(2, 4, 6)).reshape(
        channels, row_count // 2, col_count // 2 * (z_depth // 2)
    )


def upsample(values, z_depth):
    channels, row_count, length = values.shape
    col_count = length // z_depth
    shaped = values.reshape(channels, row_count, 1, col_count, 1, z_depth, 1)
    shaped = jnp.broadcast_to(shaped, (channels, row_count, 2, col_count, 2, z_depth, 2))
    return shaped.reshape(channels, 2 * row_count, 4 * col_count * z_depth)


def silu_slope(values):
    s_value = jax.nn.sigmoid(values)
    return s_value * (1.0 + values * (1.0 - s_value))


def per_device(skip_input, w_encoder, w_bottom, w_middle, w_upper, cotangent):
    top_chan = skip_input.shape[0]
    rows_fine = skip_input.shape[1]
    cols_fine = skip_input.shape[2] // Z
    rows_mid, cols_mid, depth_mid = (rows_fine // 2, cols_fine // 2, Z // 2)
    rows_low, cols_low, depth_low = (rows_fine // 4, cols_fine // 4, Z // 4)
    cells_fine = rows_fine * cols_fine * Z * lax.axis_size("gx") * lax.axis_size("gy")
    scale_fine = 1.0 / math.sqrt(cells_fine)
    scale_mid = 1.0 / math.sqrt(cells_fine // 8)
    scale_low = 1.0 / math.sqrt(cells_fine // 64)
    pool_top = pool_mean(skip_input, Z).astype(jnp.bfloat16)
    ext_pool = spatial_halo(pool_top, depth_mid, 0)
    pre_one = conv_forward(ext_pool, w_encoder, rows_mid, cols_mid, depth_mid)
    act_one = jax.nn.silu(pre_one).astype(jnp.bfloat16).reshape(-1, rows_mid, cols_mid * depth_mid)
    pool_mid = pool_mean(act_one, depth_mid).astype(jnp.bfloat16)
    col_ext = extended_2(pool_mid, (("gy", 2),), depth_low)
    whole_rows = lax.all_gather(col_ext, "gx", axis=1, tiled=True)
    ext_low = jnp.pad(whole_rows, ((0, 0), (1, 1), (0, 0)))
    rows_all = whole_rows.shape[1]
    pre_two = conv_forward(ext_low, w_bottom, rows_all, cols_low, depth_low)
    act_block = (
        jax.nn.silu(pre_two).astype(jnp.bfloat16).reshape(-1, rows_all, cols_low * depth_low)
    )
    act_two = lax.all_to_all(act_block, "gx", split_axis=1, concat_axis=0, tiled=True)
    cat_mid = jnp.concatenate([upsample(act_two, depth_low), act_one], axis=0)
    ext_mid = spatial_halo(cat_mid, depth_mid, 1)
    pre_three = conv_forward(ext_mid, w_middle, rows_mid, cols_mid, depth_mid)
    act_three = (
        jax.nn.silu(pre_three).astype(jnp.bfloat16).reshape(-1, rows_mid, cols_mid * depth_mid)
    )
    cat_top = jnp.concatenate([upsample(act_three, depth_mid), skip_input], axis=0)
    ext_top = spatial_halo(cat_top, Z, 2)
    pre_four = conv_forward(ext_top, w_upper, rows_fine, cols_fine, Z)
    features = (
        jax.nn.silu(pre_four).astype(jnp.bfloat16).reshape(top_chan, rows_fine, cols_fine * Z)
    )
    err_four = (cotangent.reshape(top_chan, -1).astype(jnp.float32) * silu_slope(pre_four)).astype(
        jnp.bfloat16
    )
    local_upper = weight_grad(ext_top, err_four, rows_fine, cols_fine, Z) * scale_fine
    dcat_top = conv_backward(
        spatial_halo(err_four.reshape(top_chan, rows_fine, cols_fine * Z), Z, 3),
        w_upper,
        rows_fine,
        cols_fine,
        Z,
    ).reshape(-1, rows_fine, cols_fine * Z)
    mid_chan = act_three.shape[0]
    err_three = (
        block_sum(dcat_top[:mid_chan], Z).reshape(mid_chan, -1) * silu_slope(pre_three)
    ).astype(jnp.bfloat16)
    local_middle = weight_grad(ext_mid, err_three, rows_mid, cols_mid, depth_mid) * scale_mid
    dcat_mid = conv_backward(
        spatial_halo(err_three.reshape(mid_chan, rows_mid, cols_mid * depth_mid), depth_mid, 4),
        w_middle,
        rows_mid,
        cols_mid,
        depth_mid,
    ).reshape(-1, rows_mid, cols_mid * depth_mid)
    low_chan = act_two.shape[0]
    dact_two = block_sum(dcat_mid[:low_chan], depth_mid)
    dact_block = lax.all_to_all(dact_two, "gx", split_axis=0, concat_axis=1, tiled=True)
    block_chan = dact_block.shape[0]
    err_two = (dact_block.reshape(block_chan, -1) * silu_slope(pre_two)).astype(jnp.bfloat16)
    part_bottom = weight_grad(ext_low, err_two, rows_all, cols_low, depth_low)
    err_grid = err_two.reshape(block_chan, rows_all, cols_low * depth_low)
    err_cols = extended_2(err_grid, (("gy", 2),), depth_low)
    err_ext = jnp.pad(err_cols, ((0, 0), (1, 1), (0, 0)))
    partial_sum = conv_backward(err_ext, w_bottom, rows_all, cols_low, depth_low).reshape(
        -1, rows_all, cols_low * depth_low
    )
    dpool_parts = lax.all_to_all(
        partial_sum.astype(jnp.bfloat16), "gx", split_axis=1, concat_axis=1, tiled=True
    ).astype(jnp.float32)
    dpool_mid = dpool_parts.reshape(
        dpool_parts.shape[0], lax.axis_size("gx"), rows_low, -1
    ).sum(axis=1)
    dact_one = dcat_mid[low_chan:] + upsample(dpool_mid, depth_low) / 8.0
    err_one = (dact_one.reshape(mid_chan, -1) * silu_slope(pre_one)).astype(jnp.bfloat16)
    local_encoder = weight_grad(ext_pool, err_one, rows_mid, cols_mid, depth_mid) * scale_mid
    (grad_encoder, grad_middle, grad_upper), grad_bottom = summed(
        (local_encoder, local_middle, local_upper), part_bottom * scale_low, 6
    )
    dpool_top = conv_backward(
        spatial_halo(err_one.reshape(mid_chan, rows_mid, cols_mid * depth_mid), depth_mid, 5),
        w_encoder,
        rows_mid,
        cols_mid,
        depth_mid,
    ).reshape(-1, rows_mid, cols_mid * depth_mid)
    grad_skip = (dcat_top[mid_chan:] + upsample(dpool_top, depth_mid) / 8.0).astype(jnp.bfloat16)
    return (features, grad_skip, grad_encoder, grad_bottom, grad_middle, grad_upper)


def solution(mesh):
    in_specs = (P(None, "gx", "gy"), P(), P("gx", None), P(), P(), P(None, "gx", "gy"))
    out_specs = (P(None, "gx", "gy"), P(None, "gx", "gy"), P(), P("gx", None), P(), P())
    return jax.shard_map(
        per_device, mesh=mesh, in_specs=in_specs, out_specs=out_specs, check_vma=False
    )
```
